512 devices in a mesh: replica: 64 (over z_lo, x, core), tensor: 8 (over z_hi, y).
Axes of the slice: x: 4, y: 4, z: 16 (z_hi: 2, z_lo: 8; z = z_hi * 8 + z_lo), core: 2. Of those that a mesh axis runs over, the one named last changes fastest.
Arguments:
- tokens: bfloat16 [16384, 4096], P('replica', 'tensor'), may hold values from -6 to 6
- norm_gain: bfloat16 [64, 4096], P('replica', 'tensor'), may hold values from 0.5 to 1.5
- key_weight: bfloat16 [64, 4096, 1024], P('replica', None, 'tensor'), may hold values from -0.09375 to 0.09375
- value_weight: bfloat16 [64, 4096, 1024], P('replica', None, 'tensor'), may hold values from -0.09375 to 0.09375
- key_cotangent: bfloat16 [16384, 1024], P('replica', 'tensor'), may hold values from -6 to 6
- value_cotangent: bfloat16 [16384, 1024], P('replica', 'tensor'), may hold values from -6 to 6
- step_index: int32 [1], replicated, may hold values from 0 to 999
Outputs:
- mixed_key: bfloat16 [64, 4096, 1024], P('replica', None, 'tensor')
- mixed_value: bfloat16 [64, 4096, 1024], P('replica', None, 'tensor')
- mixed_gain: bfloat16 [64, 4096], P('replica', 'tensor')
- input_grad: bfloat16 [16384, 4096], P('replica', 'tensor')
The draws below stay inside these ranges and needn't reach their ends.
Inputs may be any that keep to these rules, and one draw needn't show every extreme that they name: `step_index`: one training step index, the same for all replicas.
All inputs are finite; a program needn't handle non-finite values.
Results may differ from the reference program's by a relative error of at most 0.017.
Values may be sent and summed in bfloat16 or wider, within the bound.
No kernel may reach another device: no remote copies, remote signals or barrier semaphores. Data moves between devices by JAX's collectives and lax.ppermute only.
A program may use at most 64 MiB of HBM per device.

```python
import jax
import jax.numpy as jnp
from jax import lax

D = 4096
TOK = 256
KVW = 1024
TOKENS = 16384
N_REPLICA = 64
N_TENSOR = 8


def block_scale(stream_key, dims, split, low, top_value):
    def one(axis_at, blocks):
        draws = jax.random.uniform(jax.random.fold_in(jax.random.fold_in(stream_key, 6), axis_at), (blocks,), jnp.float32, low / len(split), top_value / len(split))
        return jnp.repeat(jnp.exp(draws), dims[axis_at] // blocks).reshape((-1,) + (1,) * (len(dims) - axis_at - 1))

    factor_of = one(*split[0])
    for cut in split[1:]:
        factor_of = factor_of * one(*cut)
    return factor_of


def scatter_about(own_key, extent, scale, most, split=(), dtype=jnp.bfloat16):
    entries = jax.random.normal(own_key, extent, jnp.float32) * scale
    if len(split) > 0:
        entries = block_scale(own_key, extent, split, -0.22, 0.18) * entries
    return jnp.clip(entries, min=-most, max=most).astype(dtype)


def setup_inputs(seed: int = 0) -> dict:
    streams_of = jax.random.split(jax.random.key(seed), 8)
    return {
        "tokens": scatter_about(streams_of[0], (TOKENS, D), 1.0, 6.0, ((0, 64), (1, 8))),
        "norm_gain": jnp.clip(1.0 + 0.1 * jax.random.normal(streams_of[1], (N_REPLICA, D), jnp.float32), 0.5, 1.5).astype(jnp.bfloat16),
        "key_weight": scatter_about(streams_of[2], (N_REPLICA, D, KVW), D ** -0.5, 0.09375, ((0, 64), (2, 8))),
        "value_weight": scatter_about(streams_of[3], (N_REPLICA, D, KVW), D ** -0.5, 0.09375, ((0, 64), (2, 8))),
        "key_cotangent": scatter_about(streams_of[4], (TOKENS, KVW), 1.0, 6.0, ((0, 64), (1, 8))),
        "value_cotangent": scatter_about(streams_of[5], (TOKENS, KVW), 1.0, 6.0, ((0, 64), (1, 8))),
        "step_index": jax.random.randint(streams_of[6], (1,), 0, 1000).astype(jnp.int32),
    }


lr_gain = 0.01
eps = 1e-05

def replica_step(items):
    tokens, gain, key_w, value_w, key_c, value_c = items
    lr_weight = 0.25 / TOK
    xf = tokens.astype(jnp.float32)
    gf = gain.astype(jnp.float32)
    rs = lax.rsqrt(lax.optimization_barrier(jnp.mean(xf * xf, axis=1, keepdims=True)) + eps)
    normed = (xf * rs * gf[None, :]).astype(jnp.bfloat16)
    key_step = lax.optimization_barrier(jnp.dot(normed.T, key_c, preferred_element_type=jnp.float32).astype(jnp.bfloat16))
    value_step = lax.optimization_barrier(jnp.dot(normed.T, value_c, preferred_element_type=jnp.float32).astype(jnp.bfloat16))
    width = KVW // N_TENSOR
    kc = key_c.astype(jnp.float32).reshape(TOK, N_TENSOR, width)
    vc = value_c.astype(jnp.float32).reshape(TOK, N_TENSOR, width)
    kw = key_w.astype(jnp.float32).reshape(D, N_TENSOR, width)
    vw = value_w.astype(jnp.float32).reshape(D, N_TENSOR, width)
    partial_grads = jnp.einsum('tgc,dgc->gtd', kc, kw) + jnp.einsum('tgc,dgc->gtd', vc, vw)
    partial_grads = lax.optimization_barrier(partial_grads.astype(jnp.bfloat16))
    normed_grad = lax.optimization_barrier(jnp.sum(partial_grads.astype(jnp.float32), axis=0))
    gain_step = lax.optimization_barrier(lax.optimization_barrier(jnp.sum(normed_grad * xf * rs, axis=0)).astype(jnp.bfloat16))
    centre = lax.optimization_barrier(jnp.mean(normed_grad * gf[None, :] * xf, axis=1, keepdims=True))
    input_grad = (rs * gf[None, :] * normed_grad - xf * rs * rs * rs * centre).astype(jnp.bfloat16)
    new_key = (key_w.astype(jnp.float32) - lr_weight * key_step.astype(jnp.float32)).astype(jnp.bfloat16)
    new_value = (value_w.astype(jnp.float32) - lr_weight * value_step.astype(jnp.float32)).astype(jnp.bfloat16)
    new_gain = (gf - lr_gain * gain_step.astype(jnp.float32)).astype(jnp.bfloat16)
    return (lax.optimization_barrier(new_key), lax.optimization_barrier(new_value), lax.optimization_barrier(new_gain), input_grad)

def average_pair(items):
    mine, theirs = items
    return ((mine.astype(jnp.float32) + theirs.astype(jnp.float32)) * 0.5).astype(jnp.bfloat16)

def reference(tokens, norm_gain, key_weight, value_weight, key_cotangent, value_cotangent, step_index):
    stacked = (tokens.reshape(N_REPLICA, TOK, D), norm_gain, key_weight, value_weight, key_cotangent.reshape(N_REPLICA, TOK, KVW), value_cotangent.reshape(N_REPLICA, TOK, KVW))
    new_key, new_value, new_gain, input_grad = lax.map(replica_step, stacked)
    levels = int(N_REPLICA).bit_length() - 1
    offset = jnp.left_shift(jnp.ones((), jnp.int32), jnp.mod(step_index[0], levels).astype(jnp.int32))
    mixed_key = lax.map(average_pair, (new_key, jnp.roll(new_key, -offset, axis=0)))
    mixed_value = lax.map(average_pair, (new_value, jnp.roll(new_value, -offset, axis=0)))
    mixed_gain = average_pair((new_gain, jnp.roll(new_gain, -offset, axis=0)))
    return (mixed_key, mixed_value, mixed_gain, input_grad.reshape(TOKENS, D))
```

```python
import functools

import jax
import jax.numpy as jnp
from jax import lax
from jax.experimental import pallas as pl
from jax.experimental.pallas import tpu as pltpu
from jax.sharding import PartitionSpec as P

LR_GAIN = 0.01
EPS = 1e-05
PAD = 16
F32 = jnp.float32
BF16 = jnp.bfloat16
VMEM = pl.BlockSpec(memory_space=pltpu.VMEM)


def call(body, out_shape, flops, nbytes, count):
    return pl.pallas_call(
        body,
        out_shape=out_shape,
        in_specs=[VMEM] * count,
        out_specs=jax.tree.map(lambda _: VMEM, out_shape),
        compiler_params=pltpu.CompilerParams(vmem_limit_bytes=48 * 2**20),
        cost_estimate=pl.CostEstimate(flops=flops, bytes_accessed=nbytes, transcendentals=0),
    )


def partials_kernel(ny, ck, cv, wk, wv, far, near):
    half = lax.axis_index("tensor") // ny
    cols = far.shape[2]
    c = jnp.concatenate([ck[...], cv[...]], axis=1)
    for out, side in ((far, 1 - half), (near, half)):
        for y in range(ny):
            at = pl.ds(pl.multiple_of((side * ny + y) * cols, cols), cols)
            w = jnp.concatenate([wk[0, at, :], wv[0, at, :]], axis=1)
            out[y] = lax.dot_general(c, w, (((1,), (1,)), ((), ())), preferred_element_type=F32).astype(BF16)


def weights_kernel(ny, lr, eps, *refs):
    blocks, (ck, cv, wk, wv), (nk, nv, rs_out) = refs[:-7], refs[-7:-3], refs[-3:]
    tok = ck.shape[0]
    cols = blocks[0].shape[1]
    width = ck.shape[1]
    me = lax.axis_index("tensor")
    half, y = me // ny, me % ny
    squares = jnp.zeros((tok, 1), F32)
    for b in blocks:
        x = b[:tok].astype(F32)
        squares = squares + jnp.sum(x * x, axis=1, keepdims=True)
    rs = lax.rsqrt(squares / (cols * len(blocks)) + eps)
    rs_out[...] = rs
    c = jnp.concatenate([ck[...], cv[...]], axis=1)
    for i, b in enumerate(blocks):
        side = half if i < ny else 1 - half
        owner = side * ny + (y + (ny - i % ny)) % ny
        at = pl.ds(pl.multiple_of(owner * cols, cols), cols)
        g = b[tok : tok + 1].astype(F32)
        normed = (b[:tok].astype(F32) * rs * g).astype(BF16)
        step = lax.dot_general(normed, c, (((0,), (0,)), ((), ())), preferred_element_type=F32)
        step = step.astype(BF16).astype(F32)
        nk[0, at, :] = (wk[0, at, :].astype(F32) - lr * step[:, :width]).astype(BF16)
        nv[0, at, :] = (wv[0, at, :].astype(F32) - lr * step[:, width:]).astype(BF16)


def centre_kernel(ny, *refs):
    blocks, (far, near), out = refs[:-3], refs[-3:-1], refs[-1]
    tok = far.shape[1]
    cols = blocks[0].shape[1]
    y = lax.axis_index("tensor") % ny
    total = jnp.zeros((tok, 128), F32)
    for i, b in enumerate(blocks):
        src = near if i < ny else far
        p = src[(y + (ny - i % ny)) % ny].astype(F32)
        v = p * b[tok : tok + 1].astype(F32) * b[:tok].astype(F32)
        for j in range(0, cols, 128):
            total = total + v[:, j : j + 128]
    out[...] = jnp.sum(total.T, axis=0, keepdims=True)


def finish_kernel(features, near, far, x, gain, rs, centre, grad, new_gain):
    ng = near[...].astype(F32) + far[...].astype(F32)
    xf = x[...].astype(F32)
    g = gain[...].astype(F32)
    r = rs[...]
    mean = jnp.broadcast_to(centre[...] / features, (128, centre.shape[1])).T[:, :1]
    step = jnp.sum(ng * xf * r, axis=0, keepdims=True).astype(BF16).astype(F32)
    new_gain[...] = (g - LR_GAIN * step).astype(BF16)
    grad[...] = (r * g * ng - xf * (r * r * r * mean)).astype(BF16)


def average_pair(mine, theirs):
    return ((mine.astype(F32) + theirs.astype(F32)) * 0.5).astype(BF16)


def step_at(offset, nt, nr, tokens, norm_gain, key_weight, value_weight, key_cotangent, value_cotangent):
    ny = nt // 2
    tok, cols = tokens.shape
    width = key_cotangent.shape[1]
    features = cols * nt
    lr = 0.25 / tok

    def over_tensor(a, to):
        return lax.ppermute(a, "tensor", [(i, to(i)) for i in range(nt)])

    def over_z(a):
        return over_tensor(a, lambda i: (i + ny) % nt)

    def over_y(a, k):
        return over_tensor(a, lambda i: i // ny * ny + (i + k) % ny)

    def fetch(a):
        return lax.ppermute(a, "replica", [(i, (i - offset) % nr) for i in range(nr)])

    mine = jnp.concatenate([tokens, jnp.broadcast_to(norm_gain, (PAD, cols))], axis=0)
    other = over_z(mine)
    blocks = [mine] + [over_y(mine, k) for k in range(1, ny)]
    blocks += [other] + [over_y(other, k) for k in range(1, ny)]

    half_shape = jax.ShapeDtypeStruct((ny, tok, cols), BF16)
    far, near = call(
        functools.partial(partials_kernel, ny),
        (half_shape, half_shape),
        4 * tok * features * width,
        4 * features * width + 2 * tok * features,
        4,
    )(key_cotangent, value_cotangent, key_weight, value_weight)
    groups = [list(range(ny)), list(range(ny, nt))]

    def over_y_sum(a):
        return lax.psum_scatter(a, "tensor", scatter_dimension=0, axis_index_groups=groups)

    far_sum = over_y_sum(far)
    near_sum = over_y_sum(near)
    from_far = over_z(far_sum)

    weight_shape = jax.ShapeDtypeStruct(key_weight.shape, BF16)
    new_key, new_value, rs = call(
        functools.partial(weights_kernel, ny, lr, EPS),
        (weight_shape, weight_shape, jax.ShapeDtypeStruct((tok, 1), F32)),
        4 * tok * features * width,
        8 * features * width + 2 * tok * features,
        nt + 4,
    )(*blocks, key_cotangent, value_cotangent, key_weight, value_weight)
    other_key = fetch(new_key)
    other_value = fetch(new_value)

    centre = call(
        functools.partial(centre_kernel, ny),
        jax.ShapeDtypeStruct((1, tok), F32),
        4 * tok * features,
        4 * tok * features,
        nt + 2,
    )(*blocks, far, near)
    hop = 1
    while hop < nt:
        centre = centre + over_tensor(centre, lambda i: i ^ hop)
        hop *= 2

    input_grad, new_gain = call(
        functools.partial(finish_kernel, features),
        (jax.ShapeDtypeStruct((tok, cols), BF16), jax.ShapeDtypeStruct((1, cols), BF16)),
        10 * tok * cols,
        8 * tok * cols,
        6,
    )(near_sum, from_far, tokens, norm_gain, rs, centre)
    other_gain = fetch(new_gain)
    return (
        average_pair(new_key, other_key),
        average_pair(new_value, other_value),
        average_pair(new_gain, other_gain),
        input_grad,
    )


def per_device(*args):
    nt, nr = lax.axis_size("tensor"), lax.axis_size("replica")
    levels = nr.bit_length() - 1
    level = jnp.mod(args[-1][0], levels)
    branches = [functools.partial(step_at, 2**j, nt, nr) for j in range(levels)]
    return lax.switch(level, branches, *args[:-1])


def solution(mesh):
    rows, weights = P("replica", "tensor"), P("replica", None, "tensor")
    return jax.shard_map(
        per_device,
        mesh=mesh,
        in_specs=(rows, rows, weights, weights, rows, rows, P()),
        out_specs=(weights, weights, rows, rows),
        check_vma=False,
    )
```

```python
import functools

import jax
import jax.numpy as jnp
from jax import lax
from jax.experimental import pallas as pl
from jax.experimental.pallas import tpu as pltpu
from jax.sharding import PartitionSpec as P

LR_GAIN = 0.01
EPS = 1e-05
PAD = 16
F32 = jnp.float32
BF16 = jnp.bfloat16
VMEM = pl.BlockSpec(memory_space=pltpu.VMEM)
ANY = pl.BlockSpec(memory_space=pl.ANY)
PARAMS = pltpu.CompilerParams(vmem_limit_bytes=48 * 2**20)


def call(body, out_shape, operands, flops, after=()):
    count = len(operands)

    def kernel(*refs):
        body(*refs[:count], *refs[count + len(after) :])

    moved = sum(a.size * a.dtype.itemsize for a in (*operands, *jax.tree.leaves(out_shape)))
    return pl.pallas_call(
        kernel,
        out_shape=out_shape,
        in_specs=[VMEM] * count + [ANY] * len(after),
        out_specs=jax.tree.map(lambda _: VMEM, out_shape),
        compiler_params=PARAMS,
        cost_estimate=pl.CostEstimate(flops=flops, bytes_accessed=moved, transcendentals=0),
    )(*operands, *after)


def shape(dims, dtype):
    return jax.ShapeDtypeStruct(dims, dtype)


def row_sums(terms, tok):
    total = jnp.zeros((tok, 128), F32)
    for v in terms:
        for j in range(0, v.shape[1], 128):
            total = total + v[:, j : j + 128]
    return jnp.sum(total.T, axis=0, keepdims=True)


def as_column(row):
    return jnp.broadcast_to(row, (128, row.shape[1])).T[:, :1]


def partials_kernel(ny, far, ck, cv, wk, wv, *outs):
    half, y = lax.axis_index("tensor") // ny, lax.axis_index("tensor") % ny
    c = jnp.concatenate([ck[...], cv[...]], axis=1)
    for k in range(ny):
        out = outs[k] if far else outs[0].at[k]
        cols = out.shape[1]
        owner = (1 - half) * ny + (y + k) % ny if far else half * ny + k
        at = pl.ds(pl.multiple_of(owner * cols, cols), cols)
        w = jnp.concatenate([wk[0, at, :], wv[0, at, :]], axis=1)
        out[...] = lax.dot_general(c, w, (((1,), (1,)), ((), ())), preferred_element_type=F32).astype(BF16)


def pieces(row):
    high = row.astype(BF16)
    rest = row - high.astype(F32)
    mid = rest.astype(BF16)
    return high, mid, (rest - mid.astype(F32)).astype(BF16)


def send_kernel(ny, other, near, near_parts, *refs):
    parts, (send, centre) = refs[:ny], refs[ny:]
    tok, cols = parts[0].shape
    total = sum(p[...].astype(F32) for p in parts).astype(BF16)
    send[:tok] = total
    send[tok:] = jnp.zeros((PAD, cols), BF16)

    def weighted(grad, block):
        return grad.astype(F32) * block[tok : tok + 1].astype(F32) * block[:tok].astype(F32)

    terms = [weighted(total, other)] + [weighted(near_parts[i], near.at[i]) for i in range(ny)]
    row = row_sums(terms, tok)
    centre[...] = row
    for i, piece in enumerate(pieces(row)):
        send[tok + i : tok + i + 1, :tok] = piece


def copy_kernel(a, out):
    out[...] = a[...]


def half_steps(lr, side, rs, blocks, owners, ck, cv, wk, wv, new):
    tok, width = ck.shape
    cols = blocks[0].shape[1]
    c = jnp.concatenate([ck[...], cv[...]], axis=1)
    for b, owner in zip(blocks, owners):
        here = pl.ds(pl.multiple_of(owner * cols, cols), cols)
        at = pl.ds(pl.multiple_of((side * len(blocks) + owner) * cols, cols), cols)
        normed = (b[:tok].astype(F32) * rs * b[tok : tok + 1].astype(F32)).astype(BF16)
        step = lax.dot_general(normed, c, (((0,), (0,)), ((), ())), preferred_element_type=F32)
        step = step.astype(BF16).astype(F32)
        new[0, here, :] = (wk[0, at, :].astype(F32) - lr * step[:, :width]).astype(BF16)
        new[1, here, :] = (wv[0, at, :].astype(F32) - lr * step[:, width:]).astype(BF16)


def near_kernel(ny, lr, features, near, *refs):
    far, weights, (new, rs_out) = refs[:ny], refs[ny:-2], refs[-2:]
    near = [near.at[i] for i in range(ny)]
    tok = far[0].shape[0] - PAD
    total = jnp.zeros((tok, 128), F32)
    for b in (*near, *far):
        v = b[:tok].astype(F32)
        v = v * v
        for j in range(0, v.shape[1], 128):
            total = total + v[:, j : j + 128]
    rs = lax.rsqrt(jnp.sum(total, axis=1, keepdims=True) / features + EPS)
    rs_out[...] = rs
    half_steps(lr, lax.axis_index("tensor") // ny, rs, near, range(ny), *weights, new)


def far_kernel(ny, lr, rs, *refs):
    far, weights, new = refs[:ny], refs[ny:-1], refs[-1]
    me = lax.axis_index("tensor")
    owners = [(me % ny + ny - k) % ny for k in range(ny)]
    half_steps(lr, 1 - me // ny, rs[...], far, owners, *weights, new)


def gain_kernel(near, far, x, gain, rs, new_gain):
    ng = near[...].astype(F32) + far[: near.shape[0]].astype(F32)
    step = jnp.sum(ng * x[...].astype(F32) * rs[...], axis=0, keepdims=True).astype(BF16).astype(F32)
    new_gain[...] = (gain[...].astype(F32) - LR_GAIN * step).astype(BF16)


def grad_kernel(features, near, far, x, gain, rs, *refs):
    centres, grad = refs[:-1], refs[-1]
    ng = near[...].astype(F32) + far[: near.shape[0]].astype(F32)
    xf = x[...].astype(F32)
    r = rs[...]
    mean = as_column(sum(c[...] for c in centres) / features)
    grad[...] = (r * gain[...].astype(F32) * ng - xf * (r * r * r * mean)).astype(BF16)


def average_pair(mine, theirs):
    return ((mine.astype(F32) + theirs.astype(F32)) * 0.5).astype(BF16)


def average_half(side, new, other, into, after=()):
    rows, width = new.shape[1:]
    tile = rows // 2
    first = isinstance(into[0], jax.ShapeDtypeStruct)
    extra = (*after,) if first else (*into, *after)

    def kernel(side_ref, a, b, *refs):
        for i, out in enumerate(refs[len(extra) :]):
            out[0] = average_pair(a[i], b[i])

    pair = pl.BlockSpec((2, tile, width), lambda i, s: (0, i, 0))
    whole = pl.BlockSpec((1, tile, width), lambda i, s: (0, s[0] * 2 + i, 0))
    return pl.pallas_call(
        kernel,
        out_shape=[shape(a.shape, a.dtype) for a in into],
        grid_spec=pltpu.PrefetchScalarGridSpec(
            num_scalar_prefetch=1,
            grid=(2,),
            in_specs=[pair, pair] + [ANY] * len(extra),
            out_specs=[whole, whole],
        ),
        input_output_aliases={} if first else {3: 0, 4: 1},
        compiler_params=PARAMS,
        cost_estimate=pl.CostEstimate(flops=4 * rows * width, bytes_accessed=12 * rows * width, transcendentals=0),
    )(side, new, other, *extra)


def step_at(offset, nt, nr, tokens, norm_gain, key_weight, value_weight, key_cotangent, value_cotangent):
    ny = nt // 2
    tok, cols = tokens.shape
    width = key_cotangent.shape[1]
    features = cols * nt
    lr = 0.25 / tok
    weights = (key_cotangent, value_cotangent, key_weight, value_weight)
    row = shape((1, tok), F32)

    def over_tensor(a, to):
        return lax.ppermute(a, "tensor", [(i, to(i)) for i in range(nt)])

    def over_z(a):
        return over_tensor(a, lambda i: (i + ny) % nt)

    def along_y(a, k):
        return over_tensor(a, lambda i: i // ny * ny + (i + k) % ny)

    def over_y(a):
        return [along_y(a, k) for k in range(1, ny)]

    def fetch(a):
        return lax.ppermute(a, "replica", [(i, (i - offset) % nr) for i in range(nr)])

    groups = [list(range(ny)), list(range(ny, nt))]

    def gather_y(a):
        return lax.all_gather(a, "tensor", axis_index_groups=groups)

    mine = jnp.concatenate([tokens, jnp.broadcast_to(norm_gain, (PAD, cols))], axis=0)
    other = over_z(mine)

    block, work = shape((tok, cols), BF16), 2 * tok * features * width
    far_parts = call(functools.partial(partials_kernel, ny, True), (block,) * ny, weights, work)
    near_parts = call(
        functools.partial(partials_kernel, ny, False),
        shape((ny, tok, cols), BF16),
        weights,
        work,
        after=(far_parts[0], mine),
    )
    near_sum = lax.psum_scatter(near_parts, "tensor", scatter_dimension=0, axis_index_groups=groups)
    far_parts = [far_parts[0]] + [along_y(far_parts[k], k) for k in range(1, ny)]

    near_blocks = gather_y(mine)
    send, centre = call(
        functools.partial(send_kernel, ny),
        (shape((tok + PAD, cols), BF16), shape((1, tok), F32)),
        (other, near_blocks, near_parts, *far_parts),
        6 * ny * tok * cols,
    )
    recv = over_z(send)
    again = call(copy_kernel, shape(other.shape, BF16), (other,), 0, after=(send,))
    far_blocks = (other, *over_y(again))

    half = shape((2, ny * cols, width), BF16)
    new_near, rs = call(
        functools.partial(near_kernel, ny, lr, features),
        (half, shape((tok, 1), F32)),
        (near_blocks, *far_blocks, *weights),
        2 * tok * features * width,
    )
    other_near = fetch(new_near)
    new_far = call(
        functools.partial(far_kernel, ny, lr),
        half,
        (rs, *far_blocks, *weights),
        2 * tok * features * width,
        after=(recv,),
    )
    other_far = fetch(new_far)

    centre = centre + jnp.sum(recv[tok : tok + 3, :tok].astype(F32), axis=0, keepdims=True)
    centres = (centre, *over_y(centre))

    new_gain = call(gain_kernel, shape((1, cols), BF16), (near_sum, recv, tokens, norm_gain, rs), 4 * tok * cols)
    other_gain = fetch(new_gain)
    input_grad = call(
        functools.partial(grad_kernel, features),
        shape((tok, cols), BF16),
        (near_sum, recv, tokens, norm_gain, rs, *centres),
        8 * tok * cols,
    )

    z = (lax.axis_index("tensor") // ny).astype(jnp.int32)[None]
    mixed = [shape(key_weight.shape, BF16)] * 2
    mixed = average_half(z, new_near, other_near, mixed, after=(input_grad,))
    mixed_key, mixed_value = average_half(1 - z, new_far, other_far, mixed)
    return mixed_key, mixed_value, new_gain, other_gain, input_grad


def per_device(*args):
    nt, nr = lax.axis_size("tensor"), lax.axis_size("replica")
    levels = nr.bit_length() - 1
    level = jnp.mod(args[-1][0], levels)
    branches = [functools.partial(step_at, 2**j, nt, nr) for j in range(levels)]
    mixed_key, mixed_value, new_gain, other_gain, input_grad = lax.switch(level, branches, *args[:-1])
    return mixed_key, mixed_value, average_pair(new_gain, other_gain), input_grad


def solution(mesh):
    rows, weights = P("replica", "tensor"), P("replica", None, "tensor")
    return jax.shard_map(
        per_device,
        mesh=mesh,
        in_specs=(rows, rows, weights, weights, rows, rows, P()),
        out_specs=(weights, weights, rows, rows),
        check_vma=False,
    )
```

```python
import functools

import jax
import jax.numpy as jnp
from jax import lax
from jax.experimental import pallas as pl
from jax.experimental.pallas import tpu as pltpu
from jax.sharding import PartitionSpec as P

LR_GAIN = 0.01
EPS = 1e-05
PAD = 16
F32 = jnp.float32
BF16 = jnp.bfloat16
VMEM = pl.BlockSpec(memory_space=pltpu.VMEM)
ANY = pl.BlockSpec(memory_space=pl.ANY)
PARAMS = pltpu.CompilerParams(vmem_limit_bytes=48 * 2**20)


def call(body, out_shape, operands, flops, after=()):
    count = len(operands)

    def kernel(*refs):
        body(*refs[:count], *refs[count + len(after) :])

    moved = sum(a.size * a.dtype.itemsize for a in (*operands, *jax.tree.leaves(out_shape)))
    return pl.pallas_call(
        kernel,
        out_shape=out_shape,
        in_specs=[VMEM] * count + [ANY] * len(after),
        out_specs=jax.tree.map(lambda _: VMEM, out_shape),
        compiler_params=PARAMS,
        cost_estimate=pl.CostEstimate(flops=flops, bytes_accessed=moved, transcendentals=0),
    )(*operands, *after)


def shape(dims, dtype):
    return jax.ShapeDtypeStruct(dims, dtype)


def row_sums(terms, tok):
    total = jnp.zeros((tok, 128), F32)
    for v in terms:
        for j in range(0, v.shape[1], 128):
            total = total + v[:, j : j + 128]
    return jnp.sum(total.T, axis=0, keepdims=True)


def as_column(row):
    return jnp.broadcast_to(row, (128, row.shape[1])).T[:, :1]


def partials_kernel(ny, far, ck, cv, wk, wv, *outs):
    half, y = lax.axis_index("tensor") // ny, lax.axis_index("tensor") % ny
    c = jnp.concatenate([ck[...], cv[...]], axis=1)
    for k in range(ny):
        out = outs[k] if far else outs[0].at[k]
        cols = out.shape[1]
        owner = (1 - half) * ny + (y + k) % ny if far else half * ny + k
        at = pl.ds(pl.multiple_of(owner * cols, cols), cols)
        w = jnp.concatenate([wk[0, at, :], wv[0, at, :]], axis=1)
        out[...] = lax.dot_general(c, w, (((1,), (1,)), ((), ())), preferred_element_type=F32).astype(BF16)


def pieces(row):
    high = row.astype(BF16)
    rest = row - high.astype(F32)
    mid = rest.astype(BF16)
    return high, mid, (rest - mid.astype(F32)).astype(BF16)


def send_kernel(ny, other, near, near_parts, *refs):
    parts, (send, centre) = refs[:ny], refs[ny:]
    tok, cols = parts[0].shape
    total = sum(p[...].astype(F32) for p in parts).astype(BF16)
    send[:tok] = total
    send[tok:] = jnp.zeros((PAD, cols), BF16)

    def weighted(grad, block):
        return grad.astype(F32) * block[tok : tok + 1].astype(F32) * block[:tok].astype(F32)

    terms = [weighted(total, other)] + [weighted(near_parts[i], near.at[i]) for i in range(ny)]
    row = row_sums(terms, tok)
    centre[...] = row
    for i, piece in enumerate(pieces(row)):
        send[tok + i : tok + i + 1, :tok] = piece


def block_kernel(x, gain, out):
    tok = x.shape[0]
    out[:tok] = x[...]
    out[tok:] = jnp.broadcast_to(gain[...].astype(F32), (PAD, x.shape[1])).astype(BF16)


def pair_kernel(mine, recv, out):
    tok = out.shape[1]
    out[...] = mine[...] + sum(recv[tok + i : tok + i + 1, :tok].astype(F32) for i in range(3))


def copy_kernel(a, out):
    out[...] = a[...]


def half_steps(lr, side, rs, blocks, owners, ck, cv, wk, wv, new):
    tok, width = ck.shape
    cols = blocks[0].shape[1]
    c = jnp.concatenate([ck[...], cv[...]], axis=1)
    for b, owner in zip(blocks, owners):
        here = pl.ds(pl.multiple_of(owner * cols, cols), cols)
        at = pl.ds(pl.multiple_of((side * len(blocks) + owner) * cols, cols), cols)
        normed = (b[:tok].astype(F32) * rs * b[tok : tok + 1].astype(F32)).astype(BF16)
        step = lax.dot_general(normed, c, (((0,), (0,)), ((), ())), preferred_element_type=F32)
        step = step.astype(BF16).astype(F32)
        new[0, here, :] = (wk[0, at, :].astype(F32) - lr * step[:, :width]).astype(BF16)
        new[1, here, :] = (wv[0, at, :].astype(F32) - lr * step[:, width:]).astype(BF16)


def near_kernel(ny, lr, features, near, *refs):
    far, weights, (new, rs_out) = refs[:ny], refs[ny:-2], refs[-2:]
    near = [near.at[i] for i in range(ny)]
    tok = far[0].shape[0] - PAD
    total = jnp.zeros((tok, 128), F32)
    for b in (*near, *far):
        v = b[:tok].astype(F32)
        v = v * v
        for j in range(0, v.shape[1], 128):
            total = total + v[:, j : j + 128]
    rs = lax.rsqrt(jnp.sum(total, axis=1, keepdims=True) / features + EPS)
    rs_out[...] = rs
    half_steps(lr, lax.axis_index("tensor") // ny, rs, near, range(ny), *weights, new)


def far_kernel(ny, lr, rs, *refs):
    far, weights, new = refs[:ny], refs[ny:-1], refs[-1]
    me = lax.axis_index("tensor")
    owners = [(me % ny + ny - k) % ny for k in range(ny)]
    half_steps(lr, 1 - me // ny, rs[...], far, owners, *weights, new)


def gain_kernel(near, far, x, gain, rs, new_gain):
    ng = near[...].astype(F32) + far[: near.shape[0]].astype(F32)
    step = jnp.sum(ng * x[...].astype(F32) * rs[...], axis=0, keepdims=True).astype(BF16).astype(F32)
    new_gain[...] = (gain[...].astype(F32) - LR_GAIN * step).astype(BF16)


def grad_kernel(features, near, far, x, gain, rs, *refs):
    centres, grad = refs[:-1], refs[-1]
    ng = near[...].astype(F32) + far[: near.shape[0]].astype(F32)
    xf = x[...].astype(F32)
    r = rs[...]
    mean = as_column(sum(c[...] for c in centres) / features)
    grad[...] = (r * gain[...].astype(F32) * ng - xf * (r * r * r * mean)).astype(BF16)


def average_pair(mine, theirs):
    return ((mine.astype(F32) + theirs.astype(F32)) * 0.5).astype(BF16)


def average_half(side, new, other, into, after=()):
    rows, width = new.shape[1:]
    tile = rows // 2
    first = isinstance(into[0], jax.ShapeDtypeStruct)
    extra = (*after,) if first else (*into, *after)

    def kernel(side_ref, a, b, *refs):
        for i, out in enumerate(refs[len(extra) :]):
            out[0] = average_pair(a[i], b[i])

    pair = pl.BlockSpec((2, tile, width), lambda i, s: (0, i, 0))
    whole = pl.BlockSpec((1, tile, width), lambda i, s: (0, s[0] * 2 + i, 0))
    return pl.pallas_call(
        kernel,
        out_shape=[shape(a.shape, a.dtype) for a in into],
        grid_spec=pltpu.PrefetchScalarGridSpec(
            num_scalar_prefetch=1,
            grid=(2,),
            in_specs=[pair, pair] + [ANY] * len(extra),
            out_specs=[whole, whole],
        ),
        input_output_aliases={} if first else {3: 0, 4: 1},
        compiler_params=PARAMS,
        cost_estimate=pl.CostEstimate(flops=4 * rows * width, bytes_accessed=12 * rows * width, transcendentals=0),
    )(side, new, other, *extra)


def step_at(offset, nt, nr, tokens, norm_gain, key_weight, value_weight, key_cotangent, value_cotangent):
    ny = nt // 2
    tok, cols = tokens.shape
    width = key_cotangent.shape[1]
    features = cols * nt
    lr = 0.25 / tok
    weights = (key_cotangent, value_cotangent, key_weight, value_weight)
    row = shape((1, tok), F32)

    def over_tensor(a, to):
        return lax.ppermute(a, "tensor", [(i, to(i)) for i in range(nt)])

    def over_z(a):
        return over_tensor(a, lambda i: (i + ny) % nt)

    def along_y(a, k):
        return over_tensor(a, lambda i: i // ny * ny + (i + k) % ny)

    def over_y(a):
        return [along_y(a, k) for k in range(1, ny)]

    def fetch(a):
        return lax.ppermute(a, "replica", [(i, (i - offset) % nr) for i in range(nr)])

    groups = [list(range(ny)), list(range(ny, nt))]

    def gather_y(a):
        return lax.all_gather(a, "tensor", axis_index_groups=groups)

    mine = call(block_kernel, shape((tok + PAD, cols), BF16), (tokens, norm_gain), tok * cols)
    other = over_z(mine)

    block, work = shape((tok, cols), BF16), 2 * tok * features * width
    far_parts = call(functools.partial(partials_kernel, ny, True), (block,) * ny, weights, work)
    near_parts = call(
        functools.partial(partials_kernel, ny, False),
        shape((ny, tok, cols), BF16),
        weights,
        work,
        after=(far_parts[0], mine),
    )
    near_sum = lax.psum_scatter(near_parts, "tensor", scatter_dimension=0, axis_index_groups=groups)
    far_parts = [far_parts[0]] + [along_y(far_parts[k], k) for k in range(1, ny)]

    near_blocks = gather_y(mine)
    send, centre = call(
        functools.partial(send_kernel, ny),
        (shape((tok + PAD, cols), BF16), shape((1, tok), F32)),
        (other, near_blocks, near_parts, *far_parts),
        6 * ny * tok * cols,
    )
    recv = over_z(send)
    centre = call(pair_kernel, shape((1, tok), F32), (centre, recv), 80 * tok * features * width)
    again = call(copy_kernel, shape(other.shape, BF16), (other,), 0, after=(send,))
    far_blocks = (other, *over_y(again))

    half = shape((2, ny * cols, width), BF16)
    new_near, rs = call(
        functools.partial(near_kernel, ny, lr, features),
        (half, shape((tok, 1), F32)),
        (near_blocks, *far_blocks, *weights),
        2 * tok * features * width,
        after=(centre,),
    )
    other_near = fetch(new_near)
    new_far = call(
        functools.partial(far_kernel, ny, lr),
        half,
        (rs, *far_blocks, *weights),
        2 * tok * features * width,
    )
    other_far = fetch(new_far)

    centres = (centre, *over_y(centre))

    new_gain = call(gain_kernel, shape((1, cols), BF16), (near_sum, recv, tokens, norm_gain, rs), 4 * tok * cols)
    other_gain = fetch(new_gain)
    input_grad = call(
        functools.partial(grad_kernel, features),
        shape((tok, cols), BF16),
        (near_sum, recv, tokens, norm_gain, rs, *centres),
        8 * tok * cols,
    )

    z = (lax.axis_index("tensor") // ny).astype(jnp.int32)[None]
    mixed = [shape(key_weight.shape, BF16)] * 2
    mixed = average_half(z, new_near, other_near, mixed, after=(input_grad,))
    mixed_key, mixed_value = average_half(1 - z, new_far, other_far, mixed)
    return mixed_key, mixed_value, new_gain, other_gain, input_grad


def per_device(*args):
    nt, nr = lax.axis_size("tensor"), lax.axis_size("replica")
    levels = nr.bit_length() - 1
    level = jnp.mod(args[-1][0], levels)
    branches = [functools.partial(step_at, 2**j, nt, nr) for j in range(levels)]
    mixed_key, mixed_value, new_gain, other_gain, input_grad = lax.switch(level, branches, *args[:-1])
    return mixed_key, mixed_value, average_pair(new_gain, other_gain), input_grad


def solution(mesh):
    rows, weights = P("replica", "tensor"), P("replica", None, "tensor")
    return jax.shard_map(
        per_device,
        mesh=mesh,
        in_specs=(rows, rows, weights, weights, rows, rows, P()),
        out_specs=(weights, weights, rows, rows),
        check_vma=False,
    )
```
